128 devices in a mesh: rows: 128 (over x, z, y, core).
Axes of the slice: x: 4, y: 4, z: 4, core: 2. Of those that a mesh axis runs over, the one named last changes fastest.
Arguments:
- order: int32 [1152], replicated, may hold values from 0 to 1151, as said below
- ham_cols: int32 [1152, 8], P('rows'), may hold values from -1 to 1151, as said below
- dens_cols: int32 [1152, 16], replicated, may hold values from -1 to 1151, as said below
- ham_blocks: bfloat16 [1152, 8, 128, 128], P('rows'), may hold values from -0.125 to 0.125
- coefficients: float32 [4], replicated, may hold values from 0.5 to 1.5
Outputs:
- fermi_blocks: float32 [1152, 16, 128, 128], P('rows')
The draws below stay inside these ranges and needn't reach their ends.
Inputs may be any that keep to these rules, and one draw needn't show every extreme that they name: `order`: a permutation of the block-row ids. `ham_cols`: entries of a row are distinct; each names the block row at a spatial position within 4 of the row's own, or is -1 where that position lies beyond the ends. `dens_cols`: entries of a row are distinct; each names the block row at a spatial position within 9 of the row's own, or is -1 where that position lies beyond the ends.
All inputs are finite; a program needn't handle non-finite values.
Results may differ from the reference program's by a relative error of at most 0.0022.
Values may be sent and summed in bfloat16 or wider, within the bound.
No kernel may reach another device: no remote copies, remote signals or barrier semaphores. Data moves between devices by JAX's collectives and lax.ppermute only.
A program may use at most 320 MiB of HBM per device.

```python
import jax
import jax.numpy as jnp
from jax import lax

BS = 128
KH = 8
KP = 16
TERMS = 4
REACH = 4
PREACH = 9
NB = 1152


def shared_order(key):
    return jax.random.permutation(jax.random.fold_in(key, 11), NB).astype(jnp.int32)


def pattern_ids(key, order_ids, count, reach):
    width_all = 2 * reach + 1
    offset_list = jnp.arange(width_all, dtype=jnp.int32) - reach
    scores = jax.random.randint(key, (NB, width_all), 0, 1 << 20) * width_all + jnp.arange(width_all, dtype=jnp.int32)
    scores = jnp.where(offset_list == 0, -3, jnp.where(offset_list == -1, -2, jnp.where(offset_list == 1, -1, scores)))
    chosen = jnp.argsort(scores, axis=1)[:, :count]
    offsets = offset_list[chosen]
    targets = jnp.arange(NB, dtype=jnp.int32)[:, None] + offsets
    inside = (targets >= 0) & (targets < NB)
    return jnp.where(inside, order_ids[jnp.clip(targets, 0, NB - 1)], -1).astype(jnp.int32)


def draw_order(key, part):
    return shared_order(key)


def draw_ham_cols(key, part):
    order_ids = shared_order(key)
    key = jax.random.fold_in(key, 3)
    return pattern_ids(key, order_ids, KH, REACH)


def draw_dens_cols(key, part):
    order_ids = shared_order(key)
    key = jax.random.fold_in(key, 5)
    return pattern_ids(key, order_ids, KP, PREACH)


def level_of(rng, shape, cuts, smallest, top_value):
    gain = 1.0
    for axis_at, blocks in cuts:
        heights = jax.random.uniform(jax.random.fold_in(jax.random.fold_in(rng, 6), axis_at), (blocks,), jnp.float32, smallest / len(cuts), top_value / len(cuts))
        gain = gain * jnp.repeat(jnp.exp(heights), shape[axis_at] // blocks).reshape((-1,) + (1,) * (len(shape) - 1 - axis_at))
    return gain


def gaussian(stream_key, extent, spread, limit, pieces=(), kind=jnp.bfloat16):
    array = spread * jax.random.normal(stream_key, extent, jnp.float32)
    if pieces:
        array = array * level_of(stream_key, extent, pieces, -0.22, 0.18)
    return jnp.clip(array, -limit, limit).astype(kind)


def setup_inputs(seed: int = 0) -> dict:
    arg_keys = jax.random.split(jax.random.key(seed), 6)
    order = draw_order(jax.random.fold_in(arg_keys[5], 71), 0)
    ham_cols = draw_ham_cols(jax.random.fold_in(arg_keys[5], 71), 0)
    dens_cols = draw_dens_cols(jax.random.fold_in(arg_keys[5], 71), 0)
    ham_blocks = gaussian(arg_keys[3], (NB, KH, BS, BS), (2 * KH * BS) ** -0.5, 0.125, ((0, 128),))
    coefficients = jnp.clip(jax.random.uniform(arg_keys[4], (TERMS,), jnp.float32, 0.5, 1.5), 0.5, 1.5)
    return {"order": order, "ham_cols": ham_cols, "dens_cols": dens_cols, "ham_blocks": ham_blocks, "coefficients": coefficients}


def apply_ham(window, positions, selector, ham_blocks):
    def one_row(items):
        row_pos, picks, ham_row = items
        gathered = window[row_pos].astype(jnp.float32)
        chosen = jnp.einsum('bac,bcxy->baxy', picks.astype(jnp.float32), gathered)
        return jnp.einsum('bxy,bayz->axz', ham_row.astype(jnp.float32), chosen)
    return lax.map(one_row, (positions, selector, ham_blocks))


def reference(order, ham_cols, dens_cols, ham_blocks, coefficients):
    total_rows = order.shape[0]
    block_size = ham_blocks.shape[2]
    inverse = jnp.zeros((total_rows,), jnp.int32).at[order].set(jnp.arange(total_rows, dtype=jnp.int32))
    valid = ham_cols >= 0
    positions = inverse[jnp.maximum(ham_cols, 0)].astype(jnp.int32)
    theirs = dens_cols[positions]
    live = dens_cols >= 0
    selector = (theirs[:, :, None, :] == dens_cols[:, None, :, None]) & valid[:, :, None, None] & live[:, None, :, None]
    diagonal = (dens_cols == order[:, None]).astype(jnp.float32)
    cheb_zero = diagonal[:, :, None, None] * jnp.eye(block_size, dtype=jnp.float32)
    picker = ((ham_cols[:, :, None] == dens_cols[:, None, :]) & valid[:, :, None] & live[:, None, :]).astype(jnp.float32)
    cheb_one = jnp.einsum('pba,pbxy->paxy', picker, ham_blocks.astype(jnp.float32))
    fermi = coefficients[0] * cheb_zero + coefficients[1] * cheb_one
    previous, current = cheb_zero, cheb_one
    for term in range(2, TERMS):
        rounded = current.astype(jnp.bfloat16)
        following = 2.0 * apply_ham(rounded, positions, selector, ham_blocks) - previous
        fermi = fermi + coefficients[term] * following
        previous, current = current, following
    return fermi
```

```python
import functools

import jax
import jax.numpy as jnp
from jax import lax
from jax.experimental import pallas as pl
from jax.experimental.pallas import tpu as pltpu
from jax.sharding import PartitionSpec as P

REACH = 4
PREACH = 9
BS = 128
KH = 8
KP = 16
OWN = 9
HALO = 2 * REACH
CHUNKS = (5, 2, 1)

H_ROWS = OWN + 2 * HALO
T_ROWS = OWN + 2 * REACH
COLS = 40
NO_COL = 35
FIRST_COL = REACH + PREACH
H_ZERO = H_ROWS * KH
T_ZERO = T_ROWS * KP
META = 5

VMEM = pl.BlockSpec(memory_space=pltpu.VMEM)
SMEM = pl.BlockSpec(memory_space=pltpu.SMEM)
ANY = pl.BlockSpec(memory_space=pl.ANY)


def as_blocks(ref):
    if len(ref.shape) == 3:
        return ref
    rows = ref.shape[0] // BS
    return ref.at[pl.ds(0, rows * BS)].reshape(rows, BS, BS)


def stage(copies, terms, finals, first, *refs):
    n = len(copies)
    odd_ref, coef, h_index, t_index, d_col, h_base, t_base = refs[:7]
    arrived = refs[7 : 7 + n]
    ham, cheb, part, out, sems = refs[-5:]
    odd = odd_ref[0]
    eye = (
        lax.broadcasted_iota(jnp.int32, (BS, BS), 0) == lax.broadcasted_iota(jnp.int32, (BS, BS), 1)
    ).astype(jnp.float32)
    c0, c1, c2, c3 = coef[0], coef[1], coef[2], coef[3]

    moves = []
    for i, (rows, source, even_at, odd_at) in enumerate(copies):
        blocks = rows * KH
        start = 0 if source is None else jnp.where(odd == 1, source[1], source[0]) * KH
        at = jnp.where(odd == 1, odd_at, even_at) * KH
        move = pltpu.make_async_copy(
            as_blocks(arrived[i]).at[pl.ds(start, blocks)], ham.at[pl.ds(at, blocks)], sems.at[i]
        )
        move.start()
        moves.append(move)
    if first:
        ham[H_ZERO] = jnp.zeros((BS, BS), jnp.bfloat16)
        cheb[T_ZERO] = jnp.zeros((BS, BS), jnp.bfloat16)
    for move in moves:
        move.wait()

    def row_of(low, t):
        return jnp.where(odd == 1, low + HALO + OWN - 1 + t, HALO - low - t)

    def term_row(w, own):
        j = w - REACH
        r = w - HALO
        left = jnp.concatenate([ham[w * KH + b] for b in range(KH)], axis=1)
        bases = [h_base[w * KH + b] for b in range(KH)]
        for group in range(KP // 4):
            cols = [d_col[j * KP + group * 4 + t] for t in range(4)]
            right = jnp.concatenate(
                [jnp.concatenate([ham[h_index[base + q]] for q in cols], axis=1) for base in bases],
                axis=0,
            )
            total = jnp.dot(left, right, preferred_element_type=jnp.float32)
            for t in range(4):
                q = cols[t]
                on_diagonal = (q == w + (FIRST_COL - HALO)).astype(jnp.float32)
                value = 2.0 * total[:, t * BS : (t + 1) * BS] - on_diagonal * eye
                cheb[j * KP + group * 4 + t] = value.astype(jnp.bfloat16)
                if own:
                    one = ham[h_index[w * COLS + q]].astype(jnp.float32)
                    part[r * KP + group * 4 + t] = (
                        c2 * value + (c1 - c3) * one + (c0 * on_diagonal) * eye
                    )

    def final_row(w):
        r = w - HALO
        left = jnp.concatenate([ham[w * KH + b] for b in range(KH)], axis=1)
        bases = [t_base[r * KH + b] for b in range(KH)]
        for group in range(KP // 4):
            cols = [d_col[(w - REACH) * KP + group * 4 + t] for t in range(4)]
            right = jnp.concatenate(
                [jnp.concatenate([cheb[t_index[base + q]] for q in cols], axis=1) for base in bases],
                axis=0,
            )
            total = jnp.dot(left, right, preferred_element_type=jnp.float32)
            for t in range(4):
                at = r * KP + group * 4 + t
                part[at] = part[at] + (2.0 * c3) * total[:, t * BS : (t + 1) * BS]

    def send_row(t):
        r = row_of(finals[0], t) - HALO
        return pltpu.make_async_copy(
            part.at[pl.ds(r * KP, KP)], out.at[pl.ds(r * KP, KP)], sems.at[n + t]
        )

    for low, high, own in terms:

        def make(t, _, low=low, own=own):
            term_row(row_of(low, t), own)
            return 0

        lax.fori_loop(0, high - low, make, 0)

    def finish(t, _):
        final_row(row_of(finals[0], t))
        send_row(t).start()
        return 0

    def wait(t, _):
        send_row(t).wait()
        return 0

    lax.fori_loop(0, finals[1] - finals[0], finish, 0)
    lax.fori_loop(0, finals[1] - finals[0], wait, 0)


def run_stage(copies, terms, finals, scalars, arrived, state):
    shapes = (
        pltpu.VMEM((H_ZERO + 1, BS, BS), jnp.bfloat16),
        pltpu.VMEM((T_ZERO + 1, BS, BS), jnp.bfloat16),
        pltpu.VMEM((OWN * KP, BS, BS), jnp.float32),
        jax.ShapeDtypeStruct((OWN * KP, BS, BS), jnp.float32),
    )
    n = len(arrived)
    extra = [] if state is None else list(state)
    rows = sum(high - low for low, high, _ in terms) + finals[1] - finals[0]
    return pl.pallas_call(
        functools.partial(stage, copies, terms, finals, state is None),
        out_shape=shapes,
        in_specs=[SMEM] * 7 + [ANY] * n + [VMEM, VMEM, VMEM, ANY][: len(extra)],
        out_specs=(VMEM, VMEM, VMEM, ANY),
        scratch_shapes=[pltpu.SemaphoreType.DMA((n + finals[1] - finals[0],))],
        input_output_aliases={7 + n + i: i for i in range(len(extra))},
        cost_estimate=pl.CostEstimate(
            flops=rows * KH * KP * 2 * BS**3, bytes_accessed=rows * KH * BS * BS * 2, transcendentals=0
        ),
        compiler_params=pltpu.CompilerParams(vmem_limit_bytes=8 << 20),
    )(*scalars, *arrived, *extra)


def columns_of(ids, order_window):
    found = ids[:, :, None] == order_window[None, None, :]
    places = jnp.arange(order_window.shape[0], dtype=jnp.int32) - NO_COL
    return jnp.sum(jnp.where(found, places[None, None, :], 0), axis=2) + NO_COL


def index_of(cols, spare, kept=None):
    rows, slots = cols.shape
    number = jnp.arange(rows * slots, dtype=jnp.int32).reshape(rows, slots, 1) - spare
    wanted = jnp.arange(COLS, dtype=jnp.int32)[None, None, :]
    hit = (cols[:, :, None] == wanted) & (wanted != NO_COL)
    if kept is not None:
        hit = hit & kept[:, None, :]
    table = jnp.sum(jnp.where(hit, number, 0), axis=1) + spare
    return jnp.pad(table, ((0, 1), (0, 0)), constant_values=spare).reshape(-1)


def base_of(cols, first, rows):
    return (jnp.where(cols == NO_COL, rows, cols - first) * COLS).reshape(-1)


def local(order, ham_cols, dens_cols, ham_blocks, coefficients):
    axis = "rows"
    size = lax.axis_size(axis)
    me = lax.axis_index(axis)
    odd = me & 1
    first_row = me * OWN
    near_pairs = [(i, i ^ 1) for i in range(size)]
    far_pairs = [(i, i + 1 if i % 2 else i - 1) for i in range(1, size - 1)]

    order_window = lax.dynamic_slice_in_dim(
        jnp.pad(order, (FIRST_COL, FIRST_COL), constant_values=-2), first_row, OWN + 2 * FIRST_COL, 0
    )
    dens_window = lax.dynamic_slice_in_dim(
        jnp.pad(dens_cols, ((HALO, HALO), (0, 0)), constant_values=-1), first_row, H_ROWS, 0
    )
    own_rows = jnp.arange(OWN, dtype=jnp.int32)[:, None]
    own_cols = columns_of(ham_cols, order_window)
    own_step = jnp.where(own_cols == NO_COL, 0, own_cols - (own_rows + (FIRST_COL - META)))
    all_cols = columns_of(dens_window, order_window)
    d_cols = all_cols[REACH : REACH + T_ROWS]

    blocks = ham_blocks.reshape(OWN * KH, BS, BS)
    far, k = [], 1
    for i, rows in enumerate(CHUNKS):
        start = jnp.where(odd == 1, OWN + 1 - k - rows, k - 1)
        piece = lax.dynamic_slice_in_dim(blocks, start * KH, rows * KH, 0).reshape(rows * KH * BS, BS)
        if i == 0:
            steps = lax.dynamic_slice_in_dim(own_step, jnp.where(odd == 1, 1, 0), HALO, 0)
            steps = jnp.pad(steps.astype(jnp.bfloat16), ((0, 16 - HALO), (0, BS - KH)))
            piece = jnp.concatenate([piece, steps], axis=0)
        far.append(lax.ppermute(piece, axis, far_pairs))
        k += rows
    near_blocks = lax.ppermute(blocks, axis, near_pairs)
    near_step = lax.ppermute(own_step, axis, near_pairs)

    def window_cols(far_step):
        near_rows = jnp.where(odd == 1, near_step[1:], near_step[:HALO])
        before = jnp.where(odd == 1, near_rows, far_step)
        after = jnp.where(odd == 1, far_step, near_rows)
        steps = jnp.concatenate([before, own_step, after], axis=0)
        rows = jnp.arange(H_ROWS, dtype=jnp.int32)[:, None] + (FIRST_COL - HALO - META)
        return jnp.where(steps == 0, NO_COL, steps + rows)

    odd_scalar = odd.astype(jnp.int32).reshape(1)
    t_index = index_of(d_cols, T_ZERO)
    t_base = base_of(own_cols, FIRST_COL - REACH, T_ROWS)

    wanted = jnp.arange(COLS, dtype=jnp.int32)[None, None, :]
    kept = jnp.any(all_cols[:, :, None] == wanted, axis=1)

    def scalars(far_step):
        h_cols = window_cols(far_step)
        return (
            odd_scalar,
            coefficients,
            index_of(h_cols, H_ZERO, kept),
            t_index,
            d_cols.reshape(-1),
            base_of(h_cols, FIRST_COL - HALO, H_ROWS),
            t_base,
        )

    early = scalars(jnp.zeros((HALO, KH), jnp.int32))
    state = run_stage(
        ((OWN, None, HALO, HALO), (HALO, (0, 1), HALO + OWN, 0)),
        ((-3 * REACH, -HALO, False), (-HALO, -REACH + 1, True)),
        (-HALO, -HALO + 1),
        early,
        (blocks, near_blocks),
        None,
    )
    late, k = None, 1
    for rows, piece in zip(CHUNKS, far):
        if late is None:
            steps = piece[rows * KH * BS : rows * KH * BS + HALO, :KH]
            late = scalars(steps.astype(jnp.int32))
        last = k + rows - 1
        low, high = k - REACH, last - REACH + 1
        terms = []
        if low < 1:
            terms.append((low, min(high, 1), True))
        if high > 1:
            terms.append((max(low, 1), high, False))
        state = run_stage(
            ((rows, None, HALO - last, HALO + OWN - 1 + k),),
            tuple(terms),
            (k - HALO, last - HALO + 1),
            late,
            (piece.reshape(-1, BS, BS) if piece.shape[0] % BS == 0 else piece,),
            state,
        )
        k += rows
    return state[3].reshape(OWN, KP, BS, BS)


def solution(mesh):
    return jax.shard_map(
        local,
        mesh=mesh,
        in_specs=(P(), P("rows", None), P(), P("rows", None, None, None), P()),
        out_specs=P("rows", None, None, None),
        check_vma=False,
    )
```

```python
import functools

import jax
import jax.numpy as jnp
from jax import lax
from jax.experimental import pallas as pl
from jax.experimental.pallas import tpu as pltpu
from jax.sharding import PartitionSpec as P

REACH = 4
PREACH = 9
BS = 128
KH = 8
KP = 16
OWN = 9
HALO = 2 * REACH
FIRST, SECOND = 5, 3

H_ROWS = OWN + 2 * HALO
T_ROWS = OWN + 2 * REACH
COLS = 40
NO_COL = 35
FIRST_COL = REACH + PREACH
H_ZERO = H_ROWS * KH
T_ZERO = T_ROWS * KP
META = 5
LINE = BS
T_LINES = H_ROWS + 1
LINES = T_LINES + T_ROWS + 1

VMEM = pl.BlockSpec(memory_space=pltpu.VMEM)
SMEM = pl.BlockSpec(memory_space=pltpu.SMEM)
ANY = pl.BlockSpec(memory_space=pl.ANY)


def as_blocks(ref):
    if len(ref.shape) == 3:
        return ref
    rows = ref.shape[0] // BS
    return ref.at[pl.ds(0, rows * BS)].reshape(rows, BS, BS)


def edge_lines(meta, keep, odd):
    place = lax.broadcasted_iota(jnp.int32, (16, BS), 0) == lax.broadcasted_iota(jnp.int32, (16, BS), 1)
    steps = lax.dot_general(
        meta, place.astype(jnp.bfloat16), (((0,), (0,)), ((), ())), preferred_element_type=jnp.float32
    )
    steps = jnp.where(odd, steps[:HALO], steps[1 : HALO + 1]).astype(jnp.int32)
    shift = jnp.where(odd, HALO + OWN, 0)
    row = lax.broadcasted_iota(jnp.int32, (HALO, BS), 0)
    lane = lax.broadcasted_iota(jnp.int32, (HALO, BS), 1)
    lines = jnp.full((HALO, BS), H_ZERO, jnp.int32)
    for b in range(KH):
        step = jnp.broadcast_to(steps[:, b : b + 1], (HALO, BS))
        col = jnp.where(step == 0, NO_COL, step + row + shift)
        hit = (col == lane) & (step != 0) & (keep != 0)
        lines = jnp.where(hit, row * KH + b, lines)
        w = col - (FIRST_COL - HALO)
        at = jnp.where(w < HALO, w + shift, jnp.where(w >= HALO + OWN, w - shift, w))
        at = jnp.where(step == 0, H_ROWS, at)
        lines = jnp.where(lane == COLS + b, at, lines)
    return lines


def stage(copies, passes, kind, coef, rest, *refs):
    n = len(copies)
    given, refs = refs[:1], refs[1:]
    arrived = refs[:n]
    ham, cheb, part, out, lines, table, meta, sems, table_sems = refs[-9:]
    first = kind == 0
    odd = (lax.axis_index("rows") & 1) == 1
    eye = (
        lax.broadcasted_iota(jnp.int32, (BS, BS), 0) == lax.broadcasted_iota(jnp.int32, (BS, BS), 1)
    ).astype(jnp.float32)
    c0, c1, c2, c3 = coef[0], coef[1], coef[2], coef[3]

    most = pltpu.make_async_copy(rest, table.at[pl.ds(HALO, LINES - HALO)], table_sems.at[0])
    most.start()
    if kind == 1:
        came = pltpu.make_async_copy(arrived[0].at[pl.ds(FIRST * KH * BS, 16)], meta, table_sems.at[1])
        came.start()
    moves = []
    for i, (rows, (even_from, odd_from), (even_at, odd_at)) in enumerate(copies):
        start = jnp.where(odd, odd_from, even_from) * KH
        at = jnp.where(odd, odd_at, even_at) * KH
        move = pltpu.make_async_copy(
            as_blocks(arrived[i]).at[pl.ds(start, rows * KH)], ham.at[pl.ds(at, rows * KH)], sems.at[i]
        )
        move.start()
        moves.append(move)
    if first:
        ham[H_ZERO] = jnp.zeros((BS, BS), jnp.bfloat16)
        cheb[T_ZERO] = jnp.zeros((BS, BS), jnp.bfloat16)
        lines[...] = jnp.full((HALO, BS), H_ZERO, jnp.int32)
    elif kind == 1:
        came.wait()
        lines[...] = edge_lines(meta[...], given[0][...], odd)
    else:
        lines[...] = given[0][...]
    far = pltpu.make_async_copy(lines, table.at[pl.ds(0, HALO)], table_sems.at[2])
    far.start()
    most.wait()
    far.wait()
    for move in moves:
        move.wait()

    def window_row(u):
        return jnp.where(odd, u + HALO + OWN - 1, HALO - u)

    def held_row(u):
        if u > 0:
            return jnp.where(odd, u - 1, HALO - u)
        if u <= -OWN:
            return jnp.where(odd, u + 2 * (HALO + OWN) - 1, HALO - u)
        return window_row(u)

    def term_row(u):
        w, at = window_row(u), held_row(u)
        j, r = w - REACH, w - HALO
        left = jnp.concatenate([ham[at * KH + b] for b in range(KH)], axis=1)
        bases = [table[at, COLS + b] for b in range(KH)]
        for group in range(KP // 4):
            cols = [table[T_LINES + j, COLS + group * 4 + t] for t in range(4)]
            right = jnp.concatenate(
                [jnp.concatenate([ham[table[base, q]] for q in cols], axis=1) for base in bases],
                axis=0,
            )
            total = jnp.dot(left, right, preferred_element_type=jnp.float32)
            for t in range(4):
                q = cols[t]
                on_diagonal = (q == w + (FIRST_COL - HALO)).astype(jnp.float32)
                value = 2.0 * total[:, t * BS : (t + 1) * BS] - on_diagonal * eye
                cheb[j * KP + group * 4 + t] = value.astype(jnp.bfloat16)
                if -OWN < u <= 0:
                    one = ham[table[at, q]].astype(jnp.float32)
                    part[r * KP + group * 4 + t] = (
                        c2 * value + (c1 - c3) * one + (c0 * on_diagonal) * eye
                    )

    sent = []

    def final_row(u):
        w = window_row(u)
        r = w - HALO
        left = jnp.concatenate([ham[w * KH + b] for b in range(KH)], axis=1)
        line = T_LINES + w - REACH
        bases = [table[line, COLS + KP + b] for b in range(KH)]
        for group in range(KP // 4):
            cols = [table[line, COLS + group * 4 + t] for t in range(4)]
            right = jnp.concatenate(
                [jnp.concatenate([cheb[table[base, q]] for q in cols], axis=1) for base in bases],
                axis=0,
            )
            total = jnp.dot(left, right, preferred_element_type=jnp.float32)
            for t in range(4):
                at = r * KP + group * 4 + t
                part[at] = part[at] + (2.0 * c3) * total[:, t * BS : (t + 1) * BS]
            some = pl.ds(r * KP + group * 4, 4)
            move = pltpu.make_async_copy(part.at[some], out.at[some], sems.at[n + len(sent)])
            move.start()
            sent.append(move)

    for term, low, high in passes:
        for u in range(low, high):
            if term == 2:
                term_row(u)
            else:
                final_row(u)
    for move in sent:
        move.wait()


def run_stage(copies, passes, kind, coefficients, rest, given, arrived, state):
    shapes = (
        pltpu.VMEM((H_ZERO + 1, BS, BS), jnp.bfloat16),
        pltpu.VMEM((T_ZERO + 1, BS, BS), jnp.bfloat16),
        pltpu.VMEM((OWN * KP, BS, BS), jnp.float32),
        jax.ShapeDtypeStruct((OWN * KP, BS, BS), jnp.float32),
        jax.ShapeDtypeStruct((HALO, BS), jnp.int32),
    )
    n = len(arrived)
    extra = [] if state is None else list(state[:4])
    work = sum(high - low for _, low, high in passes)
    sends = sum(high - low for term, low, high in passes if term == 3) * (KP // 4)
    return pl.pallas_call(
        functools.partial(stage, copies, passes, kind),
        out_shape=shapes,
        in_specs=[SMEM, ANY, VMEM] + [ANY] * n + [VMEM, VMEM, VMEM, ANY][: len(extra)],
        out_specs=(VMEM, VMEM, VMEM, ANY, VMEM),
        scratch_shapes=[
            pltpu.SMEM((LINES, BS), jnp.int32),
            pltpu.VMEM((16, BS), jnp.bfloat16),
            pltpu.SemaphoreType.DMA((n + sends,)),
            pltpu.SemaphoreType.DMA((3,)),
        ],
        input_output_aliases={3 + n + i: i for i in range(len(extra))},
        cost_estimate=pl.CostEstimate(
            flops=work * KH * KP * 2 * BS**3, bytes_accessed=work * KH * BS * BS * 2, transcendentals=0
        ),
        compiler_params=pltpu.CompilerParams(vmem_limit_bytes=8 << 20),
    )(coefficients, rest, given, *arrived, *extra)


def in_hbm(x):
    return pltpu.with_memory_space_constraint(x, pltpu.HBM)


def copy_edge(rows, even_from, odd_from, blocks, piece, sems):
    start = jnp.where((lax.axis_index("rows") & 1) == 1, odd_from, even_from) * (KH * BS)
    size = KH * BS
    return [
        pltpu.make_async_copy(
            blocks.at[pl.ds(start + i * size, size)], piece.at[pl.ds(i * size, size)], sems.at[i]
        )
        for i in range(rows)
    ]


def first_kernel(order_in, cols_in, blocks, piece, steps, order, cols, wide, sems):
    names = pltpu.make_async_copy(order_in, order, sems.at[FIRST])
    slots = pltpu.make_async_copy(cols_in, cols, sems.at[FIRST + 1])
    names.start()
    slots.start()
    moves = copy_edge(FIRST, 0, OWN - FIRST, blocks, piece, sems)
    for move in moves:
        move.start()
    names.wait()
    slots.wait()
    ids = cols[...]
    found = jnp.full(ids.shape, NO_COL, jnp.int32)
    for k in range(OWN + 2 * FIRST_COL):
        at = lax.axis_index("rows") * OWN + (k - FIRST_COL)
        inside = (at >= 0) & (at < order.shape[0])
        name = jnp.where(inside, order[jnp.clip(at, 0, order.shape[0] - 1)], -2)
        found = jnp.where(ids == name, k, found)
    row = lax.broadcasted_iota(jnp.int32, ids.shape, 1)
    step = jnp.where(found == NO_COL, 0, found - (row + (FIRST_COL - META)))
    steps[...] = step
    wide[...] = jnp.zeros_like(wide)
    wide[pl.ds(0, KH), pl.ds(0, OWN)] = step.astype(jnp.float32)
    piece[pl.ds(FIRST * KH * BS, 16)] = wide[...].astype(jnp.bfloat16)
    for move in moves:
        move.wait()


def pack_first(order, cols, blocks):
    size = FIRST * KH * BS
    return pl.pallas_call(
        first_kernel,
        out_shape=(pltpu.VMEM((size + 16, BS), jnp.bfloat16), jax.ShapeDtypeStruct((KH, OWN), jnp.int32)),
        in_specs=[ANY, ANY, ANY],
        out_specs=(VMEM, VMEM),
        scratch_shapes=[
            pltpu.SMEM(order.shape, jnp.int32),
            pltpu.VMEM((KH, OWN), jnp.int32),
            pltpu.VMEM((16, BS), jnp.float32),
            pltpu.SemaphoreType.DMA((FIRST + 2,)),
        ],
        cost_estimate=pl.CostEstimate(flops=0, bytes_accessed=size * BS * 2, transcendentals=0),
        compiler_params=pltpu.CompilerParams(vmem_limit_bytes=4 << 20),
    )(order, cols, blocks)


def second_kernel(blocks, after, piece, sems):
    moves = copy_edge(SECOND, FIRST, OWN - FIRST - SECOND, blocks, piece, sems)
    for move in moves:
        move.start()
    for move in moves:
        move.wait()


def pack_second(blocks, after):
    size = SECOND * KH * BS
    return pl.pallas_call(
        second_kernel,
        out_shape=pltpu.VMEM((size, BS), jnp.bfloat16),
        in_specs=[ANY, ANY],
        out_specs=VMEM,
        scratch_shapes=[pltpu.SemaphoreType.DMA((SECOND,))],
        cost_estimate=pl.CostEstimate(flops=0, bytes_accessed=size * BS * 2, transcendentals=0),
        compiler_params=pltpu.CompilerParams(vmem_limit_bytes=4 << 20),
    )(blocks, after)


def after_rows(first, last):
    return ((2, first - REACH, last - REACH + 1), (3, first - HALO, last - HALO + 1))


def columns_of(ids, order_window):
    found = ids[:, :, None] == order_window[None, None, :]
    places = jnp.arange(order_window.shape[0], dtype=jnp.int32) - NO_COL
    return jnp.sum(jnp.where(found, places[None, None, :], 0), axis=2) + NO_COL


def index_of(cols, first, spare, kept=None):
    rows, slots = cols.shape
    number = jnp.arange(rows * slots, dtype=jnp.int32).reshape(rows, slots, 1) + (first - spare)
    wanted = jnp.arange(COLS, dtype=jnp.int32)[None, None, :]
    hit = (cols[:, :, None] == wanted) & (wanted != NO_COL)
    if kept is not None:
        hit = hit & kept[:, None, :]
    return jnp.sum(jnp.where(hit, number, 0), axis=1) + spare


def local(order, ham_cols, dens_cols, ham_blocks, coefficients):
    axis = "rows"
    size = lax.axis_size(axis)
    me = lax.axis_index(axis)
    odd = (me & 1) == 1
    first_row = me * OWN
    near_pairs = [(i, i ^ 1) for i in range(size)]
    far_pairs = [(i, i + 1 if i % 2 else i - 1) for i in range(1, size - 1)]

    flat = in_hbm(ham_blocks.reshape(OWN * KH * BS, BS))
    blocks = ham_blocks.reshape(OWN * KH, BS, BS)
    piece_one, own_step = pack_first(in_hbm(order), in_hbm(ham_cols.T), flat)
    far_one = lax.ppermute(piece_one, axis, far_pairs)
    near_blocks = lax.ppermute(blocks, axis, near_pairs)
    near_step = lax.ppermute(own_step, axis, near_pairs)
    far_two = lax.ppermute(pack_second(flat, near_step), axis, far_pairs)

    order_window = lax.dynamic_slice_in_dim(
        jnp.pad(order, (FIRST_COL, FIRST_COL), constant_values=-2), first_row, OWN + 2 * FIRST_COL, 0
    )
    dens_window = lax.dynamic_slice_in_dim(
        jnp.pad(dens_cols, ((HALO, HALO), (0, 0)), constant_values=-1), first_row, H_ROWS, 0
    )
    all_cols = columns_of(dens_window, order_window)
    d_cols = all_cols[REACH : REACH + T_ROWS]
    wanted = jnp.arange(COLS, dtype=jnp.int32)[None, None, :]
    kept = jnp.any(all_cols[:, :, None] == wanted, axis=1)
    kept_near = jnp.where(odd, kept[:HALO], kept[HALO + OWN :])
    kept_far = jnp.where(odd, kept[HALO + OWN :], kept[:HALO])
    shift = (HALO + OWN) * odd.astype(jnp.int32)

    def columns(step, window):
        return jnp.where(step == 0, NO_COL, step + window)

    def lines_of(cols, first, keep):
        w = cols - (FIRST_COL - HALO)
        at = jnp.where(w < HALO, w + shift, jnp.where(w >= HALO + OWN, w - shift, w))
        named = jnp.where(cols == NO_COL, H_ROWS, at)
        lines = jnp.concatenate([index_of(cols, first * KH, H_ZERO, keep), named], axis=1)
        return jnp.pad(lines, ((0, 0), (0, LINE - COLS - KH)))

    steps = own_step.T
    own_cols = columns(steps, jnp.arange(OWN, dtype=jnp.int32)[:, None] + HALO)
    near_rows = jnp.arange(HALO, dtype=jnp.int32)[:, None] + (HALO + OWN) - shift
    near_steps = near_step.T
    near_cols = columns(jnp.where(odd, near_steps[1:], near_steps[:HALO]), near_rows)
    t_named = jnp.where(own_cols == NO_COL, T_ROWS, own_cols - (FIRST_COL - REACH)) + T_LINES
    t_lines = jnp.concatenate(
        [index_of(d_cols, 0, T_ZERO), d_cols, jnp.pad(t_named, ((REACH, REACH), (0, LINE - COLS - KP - KH)))],
        axis=1,
    )
    rest = jnp.concatenate(
        [
            lines_of(own_cols, HALO, kept[HALO : HALO + OWN]),
            lines_of(near_cols, HALO + OWN, kept_near),
            jnp.full((1, LINE), H_ZERO, jnp.int32),
            t_lines,
            jnp.full((1, LINE), T_ZERO, jnp.int32),
        ]
    )
    keep = jnp.pad(kept_far.astype(jnp.int32), ((0, 0), (0, LINE - COLS)))
    state = run_stage(
        ((OWN, (0, 0), (HALO, HALO)), (HALO, (0, 1), (HALO + OWN, HALO + OWN))),
        ((2, -3 * REACH, -REACH + 1), (3, -HALO, -HALO + 1)),
        0,
        coefficients,
        rest,
        keep,
        (in_hbm(blocks), near_blocks),
        None,
    )
    state = run_stage(
        ((FIRST, (0, 0), (HALO - FIRST, 0)),),
        after_rows(1, FIRST),
        1,
        coefficients,
        rest,
        keep,
        (far_one,),
        state,
    )
    state = run_stage(
        ((SECOND, (0, 0), (0, FIRST)),),
        after_rows(FIRST + 1, HALO),
        2,
        coefficients,
        rest,
        state[4],
        (far_two,),
        state,
    )
    return state[3].reshape(OWN, KP, BS, BS)


def solution(mesh):
    return jax.shard_map(
        local,
        mesh=mesh,
        in_specs=(P(), P("rows", None), P(), P("rows", None, None, None), P()),
        out_specs=P("rows", None, None, None),
        check_vma=False,
    )
```

```python
import functools

import jax
import jax.numpy as jnp
from jax import lax
from jax.experimental import pallas as pl
from jax.experimental.pallas import tpu as pltpu
from jax.sharding import PartitionSpec as P

REACH = 4
PREACH = 9
BS = 128
KH = 8
KP = 16
OWN = 9
HALO = 2 * REACH
FIRST, SECOND = 5, 3

H_ROWS = OWN + 2 * HALO
T_ROWS = OWN + 2 * REACH
COLS = 40
NO_COL = 35
FIRST_COL = REACH + PREACH
H_ZERO = H_ROWS * KH
T_ZERO = T_ROWS * KP
META = 5
LINE = BS
T_LINES = H_ROWS + 1
LINES = T_LINES + T_ROWS + 1

VMEM = pl.BlockSpec(memory_space=pltpu.VMEM)
SMEM = pl.BlockSpec(memory_space=pltpu.SMEM)
ANY = pl.BlockSpec(memory_space=pl.ANY)


def as_blocks(ref):
    if len(ref.shape) == 3:
        return ref
    rows = ref.shape[0] // BS
    return ref.at[pl.ds(0, rows * BS)].reshape(rows, BS, BS)


def edge_lines(meta, keep, odd):
    place = lax.broadcasted_iota(jnp.int32, (16, BS), 0) == lax.broadcasted_iota(jnp.int32, (16, BS), 1)
    steps = lax.dot_general(
        meta, place.astype(jnp.bfloat16), (((0,), (0,)), ((), ())), preferred_element_type=jnp.float32
    )
    steps = jnp.where(odd, steps[:HALO], steps[1 : HALO + 1]).astype(jnp.int32)
    shift = jnp.where(odd, HALO + OWN, 0)
    row = lax.broadcasted_iota(jnp.int32, (HALO, BS), 0)
    lane = lax.broadcasted_iota(jnp.int32, (HALO, BS), 1)
    lines = jnp.full((HALO, BS), H_ZERO, jnp.int32)
    for b in range(KH):
        step = jnp.broadcast_to(steps[:, b : b + 1], (HALO, BS))
        col = jnp.where(step == 0, NO_COL, step + row + shift)
        hit = (col == lane) & (step != 0) & (keep != 0)
        lines = jnp.where(hit, row * KH + b, lines)
        w = col - (FIRST_COL - HALO)
        at = jnp.where(w < HALO, w + shift, jnp.where(w >= HALO + OWN, w - shift, w))
        at = jnp.where(step == 0, H_ROWS, at)
        lines = jnp.where(lane == COLS + b, at, lines)
    return lines


def stage(copies, passes, kind, coef, rest, *refs):
    n = len(copies)
    given, refs = refs[:1], refs[1:]
    arrived = refs[:n]
    ham, cheb, part, out, table, lines, made, meta, sems, table_sems = refs[-10:]
    first = kind == 0
    odd = (lax.axis_index("rows") & 1) == 1
    eye = (
        lax.broadcasted_iota(jnp.int32, (BS, BS), 0) == lax.broadcasted_iota(jnp.int32, (BS, BS), 1)
    ).astype(jnp.float32)
    c0, c1, c2, c3 = coef[0], coef[1], coef[2], coef[3]

    if first:
        most = pltpu.make_async_copy(rest, table.at[pl.ds(HALO, LINES - HALO)], table_sems.at[0])
        most.start()
    if kind == 1:
        came = pltpu.make_async_copy(arrived[0].at[pl.ds(FIRST * KH * BS, 16)], meta, table_sems.at[1])
        came.start()
    moves = []
    for i, (rows, (even_from, odd_from), (even_at, odd_at)) in enumerate(copies):
        start = jnp.where(odd, odd_from, even_from) * KH
        at = jnp.where(odd, odd_at, even_at) * KH
        move = pltpu.make_async_copy(
            as_blocks(arrived[i]).at[pl.ds(start, rows * KH)], ham.at[pl.ds(at, rows * KH)], sems.at[i]
        )
        move.start()
        moves.append(move)
    if first:
        ham[H_ZERO] = jnp.zeros((BS, BS), jnp.bfloat16)
        cheb[T_ZERO] = jnp.zeros((BS, BS), jnp.bfloat16)
    elif kind == 1:
        came.wait()
        lines[...] = edge_lines(meta[...], given[0][...], odd)
        far = pltpu.make_async_copy(lines, table.at[pl.ds(0, HALO)], table_sems.at[2])
        far.start()
        far.wait()
    if first:
        most.wait()
    for move in moves:
        move.wait()

    def window_row(u):
        return jnp.where(odd, u + HALO + OWN - 1, HALO - u)

    def held_row(u):
        if u > 0:
            return jnp.where(odd, u - 1, HALO - u)
        if u <= -OWN:
            return jnp.where(odd, u + 2 * (HALO + OWN) - 1, HALO - u)
        return window_row(u)

    def term_row(u):
        w, at = window_row(u), held_row(u)
        j, r = w - REACH, w - HALO
        left = jnp.concatenate([ham[at * KH + b] for b in range(KH)], axis=1)
        bases = [table[at, COLS + b] for b in range(KH)]
        for group in range(KP // 4):
            cols = [table[T_LINES + j, COLS + group * 4 + t] for t in range(4)]
            right = jnp.concatenate(
                [jnp.concatenate([ham[table[base, q]] for q in cols], axis=1) for base in bases],
                axis=0,
            )
            total = jnp.dot(left, right, preferred_element_type=jnp.float32)
            for t in range(4):
                q = cols[t]
                on_diagonal = (q == w + (FIRST_COL - HALO)).astype(jnp.float32)
                value = 2.0 * total[:, t * BS : (t + 1) * BS] - on_diagonal * eye
                cheb[j * KP + group * 4 + t] = value.astype(jnp.bfloat16)
                if -OWN < u <= 0:
                    one = ham[table[at, q]].astype(jnp.float32)
                    part[r * KP + group * 4 + t] = (
                        c2 * value + (c1 - c3) * one + (c0 * on_diagonal) * eye
                    )

    sent = []

    def final_row(u):
        w = window_row(u)
        r = w - HALO
        left = jnp.concatenate([ham[w * KH + b] for b in range(KH)], axis=1)
        line = T_LINES + w - REACH
        bases = [table[line, COLS + KP + b] for b in range(KH)]
        for group in range(KP // 4):
            cols = [table[line, COLS + group * 4 + t] for t in range(4)]
            right = jnp.concatenate(
                [jnp.concatenate([cheb[table[base, q]] for q in cols], axis=1) for base in bases],
                axis=0,
            )
            total = jnp.dot(left, right, preferred_element_type=jnp.float32)
            for t in range(4):
                at = r * KP + group * 4 + t
                made[len(sent) * KP + group * 4 + t] = part[at] + (2.0 * c3) * total[:, t * BS : (t + 1) * BS]
        move = pltpu.make_async_copy(
            made.at[pl.ds(len(sent) * KP, KP)], out.at[pl.ds(r * KP, KP)], sems.at[n + len(sent)]
        )
        move.start()
        sent.append(move)

    for term, low, high in passes:
        for u in range(low, high):
            if term == 2:
                term_row(u)
            else:
                final_row(u)
    for move in sent:
        move.wait()


def run_stage(copies, passes, kind, coefficients, rest, given, arrived, state):
    shapes = (
        pltpu.VMEM((H_ZERO + 1, BS, BS), jnp.bfloat16),
        pltpu.VMEM((T_ZERO + 1, BS, BS), jnp.bfloat16),
        pltpu.VMEM((OWN * KP, BS, BS), jnp.float32),
        jax.ShapeDtypeStruct((OWN * KP, BS, BS), jnp.float32),
        pltpu.SMEM((LINES, BS), jnp.int32),
    )
    n = len(arrived)
    extra = [] if state is None else list(state)
    work = sum(high - low for _, low, high in passes)
    finals = sum(high - low for term, low, high in passes if term == 3)
    return pl.pallas_call(
        functools.partial(stage, copies, passes, kind),
        out_shape=shapes,
        in_specs=[SMEM, ANY, VMEM] + [ANY] * n + [VMEM, VMEM, VMEM, ANY, SMEM][: len(extra)],
        out_specs=(VMEM, VMEM, VMEM, ANY, SMEM),
        scratch_shapes=[
            pltpu.VMEM((HALO, BS), jnp.int32),
            pltpu.VMEM((max(finals, 1) * KP, BS, BS), jnp.float32),
            pltpu.VMEM((16, BS), jnp.bfloat16),
            pltpu.SemaphoreType.DMA((n + finals,)),
            pltpu.SemaphoreType.DMA((3,)),
        ],
        input_output_aliases={3 + n + i: i for i in range(len(extra))},
        cost_estimate=pl.CostEstimate(
            flops=work * KH * KP * 2 * BS**3, bytes_accessed=work * KH * BS * BS * 2, transcendentals=0
        ),
        compiler_params=pltpu.CompilerParams(vmem_limit_bytes=12 << 20),
    )(coefficients, rest, given, *arrived, *extra)


def in_hbm(x):
    return pltpu.with_memory_space_constraint(x, pltpu.HBM)


def copy_edge(rows, even_from, odd_from, blocks, piece, sems):
    start = jnp.where((lax.axis_index("rows") & 1) == 1, odd_from, even_from) * (KH * BS)
    size = KH * BS
    return [
        pltpu.make_async_copy(
            blocks.at[pl.ds(start + i * size, size)], piece.at[pl.ds(i * size, size)], sems.at[i]
        )
        for i in range(rows)
    ]


def first_kernel(order_in, cols_in, coef_in, blocks, piece, steps, window, coef, order, cols, wide, sems):
    names = pltpu.make_async_copy(order_in, order, sems.at[FIRST])
    slots = pltpu.make_async_copy(cols_in, cols, sems.at[FIRST + 1])
    scales = pltpu.make_async_copy(coef_in, coef, sems.at[FIRST + 2])
    names.start()
    slots.start()
    scales.start()
    moves = copy_edge(FIRST, 0, OWN - FIRST, blocks, piece, sems)
    for move in moves:
        move.start()
    names.wait()
    slots.wait()
    ids = cols[...]
    found = jnp.full(ids.shape, NO_COL, jnp.int32)
    lane = lax.broadcasted_iota(jnp.int32, window.shape, 1)
    names_here = jnp.full(window.shape, -2, jnp.int32)
    for k in range(OWN + 2 * FIRST_COL):
        at = lax.axis_index("rows") * OWN + (k - FIRST_COL)
        inside = (at >= 0) & (at < order.shape[0])
        name = jnp.where(inside, order[jnp.clip(at, 0, order.shape[0] - 1)], -2)
        found = jnp.where(ids == name, k, found)
        names_here = jnp.where(lane == k, name, names_here)
    window[...] = names_here
    row = lax.broadcasted_iota(jnp.int32, ids.shape, 1)
    step = jnp.where(found == NO_COL, 0, found - (row + (FIRST_COL - META)))
    steps[...] = step
    wide[...] = jnp.zeros_like(wide)
    wide[pl.ds(0, KH), pl.ds(0, OWN)] = step.astype(jnp.float32)
    piece[pl.ds(FIRST * KH * BS, 16)] = wide[...].astype(jnp.bfloat16)
    scales.wait()
    for move in moves:
        move.wait()


def pack_first(order, cols, coefficients, blocks):
    size = FIRST * KH * BS
    return pl.pallas_call(
        first_kernel,
        out_shape=(
            pltpu.VMEM((size + 16, BS), jnp.bfloat16),
            jax.ShapeDtypeStruct((KH, OWN), jnp.int32),
            jax.ShapeDtypeStruct((8, BS), jnp.int32),
            pltpu.SMEM(coefficients.shape, jnp.float32),
        ),
        in_specs=[ANY, ANY, ANY, ANY],
        out_specs=(VMEM, VMEM, VMEM, SMEM),
        scratch_shapes=[
            pltpu.SMEM(order.shape, jnp.int32),
            pltpu.VMEM((KH, OWN), jnp.int32),
            pltpu.VMEM((16, BS), jnp.float32),
            pltpu.SemaphoreType.DMA((FIRST + 3,)),
        ],
        cost_estimate=pl.CostEstimate(flops=0, bytes_accessed=size * BS * 2, transcendentals=0),
        compiler_params=pltpu.CompilerParams(vmem_limit_bytes=4 << 20),
    )(order, cols, coefficients, blocks)


def second_kernel(blocks, after, piece, sems):
    moves = copy_edge(SECOND, FIRST, OWN - FIRST - SECOND, blocks, piece, sems)
    for move in moves:
        move.start()
    for move in moves:
        move.wait()


def pack_second(blocks, after):
    size = SECOND * KH * BS
    return pl.pallas_call(
        second_kernel,
        out_shape=pltpu.VMEM((size, BS), jnp.bfloat16),
        in_specs=[ANY, ANY],
        out_specs=VMEM,
        scratch_shapes=[pltpu.SemaphoreType.DMA((SECOND,))],
        cost_estimate=pl.CostEstimate(flops=0, bytes_accessed=size * BS * 2, transcendentals=0),
        compiler_params=pltpu.CompilerParams(vmem_limit_bytes=4 << 20),
    )(blocks, after)


def after_rows(first, last):
    return ((2, first - REACH, last - REACH + 1), (3, first - HALO, last - HALO + 1))


def columns_of(ids, order_window):
    found = ids[:, :, None] == order_window[None, None, :]
    places = jnp.arange(order_window.shape[0], dtype=jnp.int32) - NO_COL
    return jnp.sum(jnp.where(found, places[None, None, :], 0), axis=2) + NO_COL


def index_of(cols, first, spare, kept=None):
    rows, slots = cols.shape
    number = jnp.arange(rows * slots, dtype=jnp.int32).reshape(rows, slots, 1) + (first - spare)
    wanted = jnp.arange(COLS, dtype=jnp.int32)[None, None, :]
    hit = (cols[:, :, None] == wanted) & (wanted != NO_COL)
    if kept is not None:
        hit = hit & kept[:, None, :]
    return jnp.sum(jnp.where(hit, number, 0), axis=1) + spare


def local(order, ham_cols, dens_cols, ham_blocks, coefficients):
    axis = "rows"
    size = lax.axis_size(axis)
    me = lax.axis_index(axis)
    odd = (me & 1) == 1
    first_row = me * OWN
    near_pairs = [(i, i ^ 1) for i in range(size)]
    far_pairs = [(i, i + 1 if i % 2 else i - 1) for i in range(1, size - 1)]

    flat = in_hbm(ham_blocks.reshape(OWN * KH * BS, BS))
    blocks = ham_blocks.reshape(OWN * KH, BS, BS)
    piece_one, own_step, window, scales = pack_first(
        in_hbm(order), in_hbm(ham_cols.T), in_hbm(coefficients), flat
    )
    far_one = lax.ppermute(piece_one, axis, far_pairs)
    near_blocks = lax.ppermute(blocks, axis, near_pairs)
    near_step = lax.ppermute(own_step, axis, near_pairs)
    far_two = lax.ppermute(pack_second(flat, near_step), axis, far_pairs)

    order_window = window[0, : OWN + 2 * FIRST_COL]
    dens_window = lax.dynamic_slice_in_dim(
        jnp.pad(dens_cols, ((HALO, HALO), (0, 0)), constant_values=-1), first_row, H_ROWS, 0
    )
    all_cols = columns_of(dens_window, order_window)
    d_cols = all_cols[REACH : REACH + T_ROWS]
    wanted = jnp.arange(COLS, dtype=jnp.int32)[None, None, :]
    kept = jnp.any(all_cols[:, :, None] == wanted, axis=1)
    kept_near = jnp.where(odd, kept[:HALO], kept[HALO + OWN :])
    kept_far = jnp.where(odd, kept[HALO + OWN :], kept[:HALO])
    shift = (HALO + OWN) * odd.astype(jnp.int32)

    def columns(step, window):
        return jnp.where(step == 0, NO_COL, step + window)

    def lines_of(cols, first, keep):
        w = cols - (FIRST_COL - HALO)
        at = jnp.where(w < HALO, w + shift, jnp.where(w >= HALO + OWN, w - shift, w))
        named = jnp.where(cols == NO_COL, H_ROWS, at)
        lines = jnp.concatenate([index_of(cols, first * KH, H_ZERO, keep), named], axis=1)
        return jnp.pad(lines, ((0, 0), (0, LINE - COLS - KH)))

    steps = own_step.T
    own_cols = columns(steps, jnp.arange(OWN, dtype=jnp.int32)[:, None] + HALO)
    near_rows = jnp.arange(HALO, dtype=jnp.int32)[:, None] + (HALO + OWN) - shift
    near_steps = near_step.T
    near_cols = columns(jnp.where(odd, near_steps[1:], near_steps[:HALO]), near_rows)
    t_named = jnp.where(own_cols == NO_COL, T_ROWS, own_cols - (FIRST_COL - REACH)) + T_LINES
    t_lines = jnp.concatenate(
        [index_of(d_cols, 0, T_ZERO), d_cols, jnp.pad(t_named, ((REACH, REACH), (0, LINE - COLS - KP - KH)))],
        axis=1,
    )
    rest = jnp.concatenate(
        [
            lines_of(own_cols, HALO, kept[HALO : HALO + OWN]),
            lines_of(near_cols, HALO + OWN, kept_near),
            jnp.full((1, LINE), H_ZERO, jnp.int32),
            t_lines,
            jnp.full((1, LINE), T_ZERO, jnp.int32),
        ]
    )
    keep = jnp.pad(kept_far.astype(jnp.int32), ((0, 0), (0, LINE - COLS)))
    state = run_stage(
        ((OWN, (0, 0), (HALO, HALO)), (HALO, (0, 1), (HALO + OWN, HALO + OWN))),
        ((2, -3 * REACH, -REACH + 1), (3, -HALO, -HALO + 1)),
        0,
        scales,
        rest,
        keep,
        (in_hbm(blocks), near_blocks),
        None,
    )
    state = run_stage(
        ((FIRST, (0, 0), (HALO - FIRST, 0)),),
        after_rows(1, FIRST),
        1,
        scales,
        rest,
        keep,
        (far_one,),
        state,
    )
    state = run_stage(
        ((SECOND, (0, 0), (0, FIRST)),),
        after_rows(FIRST + 1, HALO),
        2,
        scales,
        rest,
        keep,
        (far_two,),
        state,
    )
    return state[3].reshape(OWN, KP, BS, BS)


def solution(mesh):
    return jax.shard_map(
        local,
        mesh=mesh,
        in_specs=(P(), P("rows", None), P(), P("rows", None, None, None), P()),
        out_specs=P("rows", None, None, None),
        check_vma=False,
    )
```
